32 devices in a mesh: dp: 16 (over z, y, core), rows: 2 (over x).
Axes of the slice: x: 2, y: 2, z: 4, core: 2. Of those that a mesh axis runs over, the one named last changes fastest.
Arguments:
- features: bfloat16 [16, 32, 32, 768], P('dp', 'rows'), may hold values from -6 to 6
- bucket: int32 [16], P('dp'), may hold values from 0 to 16, as said below
- kernel: float32 [7, 7, 768], replicated, may hold values from -0.875 to 0.875
- up_weight: bfloat16 [768, 2816], P('dp'), may hold values from -0.21875 to 0.21875
- down_weight: bfloat16 [2816, 768], P('dp'), may hold values from -0.109375 to 0.109375
- cotangent: bfloat16 [16, 32, 32, 768], P('dp', 'rows'), may hold values from -6 to 6
Outputs:
- block_out: bfloat16 [16, 32, 32, 768], P('dp', 'rows')
- feature_grad: bfloat16 [16, 32, 32, 768], P('dp', 'rows')
- up_grad: float32 [768, 2816], P('dp')
- down_grad: float32 [2816, 768], P('dp')
- kernel_grad: float32 [7, 7, 768], replicated
The draws below stay inside these ranges and needn't reach their ends.
Inputs may be any that keep to these rules, and one draw needn't show every extreme that they name: `bucket`: both ends of the range occur in every draw.
All inputs are finite; a program needn't handle non-finite values.
Results may differ from the reference program's by a relative error of at most 0.0075.
Values may be sent and summed in bfloat16 or wider, within the bound.
A program may use at most 128 MiB of HBM per device.

```python
import jax
import jax.numpy as jnp
from jax import lax

C = 768
HID = 2816
KS = 7
CH = 32
CW = 32
IMAGES = 16
AREA = 512


def draw_bucket(key, part):
    first_key, second_key = jax.random.split(jax.random.fold_in(key, 11))
    drawn = jax.random.randint(first_key, (IMAGES,), 0, CH // 2 + 1)
    ranking = jax.random.permutation(second_key, IMAGES)
    drawn = jnp.where(ranking == 0, 0, drawn)
    drawn = jnp.where(ranking == 1, CH // 2, drawn)
    return drawn.astype(jnp.int32)


def strengthened(values, own_key, source, target, parts, factor):
    owner, partner = [(jnp.arange(values.shape[dim]) // (values.shape[dim] // parts)).reshape([-1 if axis == dim else 1 for axis in range(values.ndim)]) for dim in (source, target)]
    chosen = jax.random.permutation(own_key, parts)[partner]
    strong = (owner == chosen) | (owner == (partner + parts // 2) % parts)
    return jnp.where(strong, factor * values, values)


def level_of(stream_key, extent, cuts, least, high):
    gain, own = 1.0, jax.random.fold_in(stream_key, 6)
    for axis_at, shards_of in cuts:
        draws = jnp.exp(jax.random.uniform(jax.random.fold_in(own, axis_at), (shards_of,), jnp.float32, least / len(cuts), high / len(cuts)))
        gain = gain * jnp.repeat(draws, extent[axis_at] // shards_of).reshape([-1 if axis == axis_at else 1 for axis in range(len(extent))])
    return gain


def centred(key, extent, spread, most, cuts=(), held_as=jnp.bfloat16):
    array = jax.random.normal(key, extent, jnp.float32) * spread
    if len(cuts) > 0:
        array = level_of(key, extent, cuts, -0.22, 0.18) * array
    return jnp.clip(array, min=-most, max=most).astype(held_as)


def heavy_noise(stream_key, dims, deviation, most, cuts, heavy, held_as=jnp.bfloat16):
    values = deviation * jax.random.normal(stream_key, dims, jnp.float32)
    if cuts:
        values = values * level_of(stream_key, dims, cuts, -0.22, 0.18)
    return jnp.clip(strengthened(values, jax.random.fold_in(stream_key, 3), *heavy), -most, most).astype(held_as)


def setup_inputs(seed: int = 0) -> dict:
    key_list = jax.random.split(jax.random.key(seed), 7)
    return {
        "features": heavy_noise(key_list[0], (IMAGES, CH, CW, C), 1.0, 6.0, ((0, 16), (1, 2)), (0, 3, 16, 2.0)),
        "bucket": draw_bucket(jax.random.fold_in(key_list[6], 71), 0),
        "kernel": centred(key_list[2], (KS, KS, C), (KS * KS) ** -0.5, 0.875, (), jnp.float32),
        "up_weight": centred(key_list[3], (C, HID), C ** -0.5, 0.21875, ((0, 16),)),
        "down_weight": centred(key_list[4], (HID, C), HID ** -0.5, 0.109375, ((0, 16),)),
        "cotangent": centred(key_list[5], (IMAGES, CH, CW, C), 1.0, 6.0, ((0, 16), (1, 2))),
    }


INV_ROOT_TWO = 0.7071067811865476
INV_ROOT_TAU = 0.3989422804014327
EPSILON = 1e-06

def gelu_parts(pre_act):
    normal_cdf = 0.5 * (1.0 + lax.erf(pre_act * INV_ROOT_TWO))
    density = jnp.exp(-0.5 * pre_act * pre_act) * INV_ROOT_TAU
    return (pre_act * normal_cdf, normal_cdf + pre_act * density)

def depthwise(padded, kernel, out_rows, out_cols, flipped):
    span = kernel.shape[0]
    result = jnp.zeros(padded.shape[:-3] + (out_rows, out_cols, padded.shape[-1]), jnp.float32)
    for offset_row in range(span):
        for offset_col in range(span):
            start_row = span - 1 - offset_row if flipped else offset_row
            start_col = span - 1 - offset_col if flipped else offset_col
            result = result + kernel[offset_row, offset_col] * padded[..., start_row:start_row + out_rows, start_col:start_col + out_cols, :]
    return result

def kernel_terms(grad_conv, padded, span):
    reduce_axes = tuple(range(grad_conv.ndim - 1))
    rows_out = grad_conv.shape[-3]
    cols_out = grad_conv.shape[-2]
    kernel_rows = []
    for offset_row in range(span):
        kernel_row = []
        for offset_col in range(span):
            window = padded[..., offset_row:offset_row + rows_out, offset_col:offset_col + cols_out, :]
            kernel_row.append(lax.optimization_barrier(jnp.sum(grad_conv * window, axis=reduce_axes)))
        kernel_rows.append(jnp.stack(kernel_row))
    return jnp.stack(kernel_rows)

def layer_norm(convolved):
    centered = convolved - lax.optimization_barrier(jnp.mean(convolved, axis=-1, keepdims=True))
    inv_std = lax.rsqrt(lax.optimization_barrier(jnp.mean(centered * centered, axis=-1, keepdims=True)) + EPSILON)
    return (centered * inv_std, inv_std)

def norm_backward(grad_norm, unit_norm, inv_std):
    first_mean = lax.optimization_barrier(jnp.mean(grad_norm, axis=-1, keepdims=True))
    second_mean = lax.optimization_barrier(jnp.mean(grad_norm * unit_norm, axis=-1, keepdims=True))
    return inv_std * (grad_norm - first_mean - unit_norm * second_mean)

def pointwise(tokens, cot_rows, up_full, down_full):
    pre_act = jnp.dot(tokens, up_full, preferred_element_type=jnp.float32)
    hidden, derivative = gelu_parts(pre_act)
    activation = hidden.astype(jnp.bfloat16)
    branch = jnp.dot(activation, down_full, preferred_element_type=jnp.float32)
    grad_act = lax.dot_general(cot_rows, down_full, (((1,), (1,)), ((), ())), preferred_element_type=jnp.float32)
    grad_pre = (grad_act * derivative).astype(jnp.bfloat16)
    grad_norm = lax.dot_general(grad_pre, up_full, (((1,), (1,)), ((), ())), preferred_element_type=jnp.float32)
    return (activation, branch, grad_pre, grad_norm)

def reference(features, bucket, kernel, up_weight, down_weight, cotangent):
    reach = KS // 2

    def one_image(carry, inputs):
        feature_one, cot_one, bucket_one = inputs
        image_rows = CH // 2 + bucket_one
        image_cols = jnp.minimum(CW, AREA // image_rows)
        inside = (jnp.arange(CH, dtype=jnp.int32)[:, None] < image_rows) & (jnp.arange(CW, dtype=jnp.int32)[None, :] < image_cols)
        inside_cells = inside[:, :, None]
        masked = jnp.where(inside_cells, feature_one, jnp.zeros((), feature_one.dtype))
        masked_cot = jnp.where(inside_cells, cot_one, jnp.zeros((), cot_one.dtype))
        padded = jnp.pad(masked, ((reach, reach), (reach, reach), (0, 0)))
        convolved = jnp.where(inside_cells, depthwise(padded, kernel, CH, CW, False), 0.0)
        unit_norm, inv_std = layer_norm(convolved)
        normed = unit_norm.astype(jnp.bfloat16)
        tokens = normed.reshape(CH * CW, C)
        cot_rows = masked_cot.reshape(CH * CW, C)
        activation, branch, grad_pre, grad_norm = pointwise(tokens, cot_rows, up_weight, down_weight)
        block_out = (masked + branch.reshape(CH, CW, C)).astype(jnp.bfloat16)
        down_term = lax.dot_general(activation, cot_rows, (((0,), (0,)), ((), ())), preferred_element_type=jnp.float32)
        up_term = lax.dot_general(tokens, grad_pre, (((0,), (0,)), ((), ())), preferred_element_type=jnp.float32)
        grad_conv = jnp.where(inside_cells, norm_backward(grad_norm.reshape(CH, CW, C), unit_norm, inv_std), 0.0)
        kernel_term = kernel_terms(grad_conv, padded, KS)
        grad_padded = jnp.pad(grad_conv, ((reach, reach), (reach, reach), (0, 0)))
        feature_grad = jnp.where(inside_cells, masked_cot + depthwise(grad_padded, kernel, CH, CW, True), 0.0).astype(jnp.bfloat16)
        new_carry = (carry[0] + down_term, carry[1] + up_term, carry[2] + kernel_term)
        return (new_carry, (block_out, feature_grad))
    start = (jnp.zeros((HID, C), jnp.float32), jnp.zeros((C, HID), jnp.float32), jnp.zeros((KS, KS, C), jnp.float32))
    totals, outputs = lax.scan(one_image, start, (features, cotangent, bucket))
    block_out, feature_grad = outputs
    return (block_out, feature_grad, totals[1] / IMAGES, totals[0] / IMAGES, totals[2] / IMAGES)
```

```python
import jax
import jax.numpy as jnp
from jax import lax
from jax.sharding import PartitionSpec as P

INV_ROOT_TWO = 0.7071067811865476
INV_ROOT_TAU = 0.3989422804014327
EPSILON = 1e-06


def padded_2(block, sides, width):
    for axis, dim in sides:
        count = lax.axis_size(axis)
        forward = [(i, i + 1) for i in range(count - 1)]
        backward = [(target, source) for source, target in forward]
        low = lax.ppermute(
            lax.slice_in_dim(block, block.shape[dim] - width, None, axis=dim), axis, forward
        )
        high = lax.ppermute(lax.slice_in_dim(block, 0, width, axis=dim), axis, backward)
        block = jnp.concatenate([low, block, high], axis=dim)
    return block


def gelu_parts(pre_act):
    normal_cdf = 0.5 * (1.0 + lax.erf(pre_act * INV_ROOT_TWO))
    density = jnp.exp(-0.5 * pre_act * pre_act) * INV_ROOT_TAU
    return (pre_act * normal_cdf, normal_cdf + pre_act * density)


def depthwise(padded, kernel, out_rows, out_cols, flipped):
    span = kernel.shape[0]
    result = jnp.zeros(padded.shape[:-3] + (out_rows, out_cols, padded.shape[-1]), jnp.float32)
    for offset_row in range(span):
        for offset_col in range(span):
            start_row = span - 1 - offset_row if flipped else offset_row
            start_col = span - 1 - offset_col if flipped else offset_col
            result = (
                result
                + kernel[offset_row, offset_col]
                * padded[..., start_row : start_row + out_rows, start_col : start_col + out_cols, :]
            )
    return result


def kernel_terms(grad_conv, padded, span):
    reduce_axes = tuple(range(grad_conv.ndim - 1))
    rows_out = grad_conv.shape[-3]
    cols_out = grad_conv.shape[-2]
    kernel_rows = []
    for offset_row in range(span):
        kernel_row = []
        for offset_col in range(span):
            window = padded[
                ..., offset_row : offset_row + rows_out, offset_col : offset_col + cols_out, :
            ]
            kernel_row.append(jnp.sum(grad_conv * window, axis=reduce_axes))
        kernel_rows.append(jnp.stack(kernel_row))
    return jnp.stack(kernel_rows)


def layer_norm(convolved):
    centered = convolved - jnp.mean(convolved, axis=-1, keepdims=True)
    inv_std = lax.rsqrt(jnp.mean(centered * centered, axis=-1, keepdims=True) + EPSILON)
    return (centered * inv_std, inv_std)


def norm_backward(grad_norm, unit_norm, inv_std):
    first_mean = jnp.mean(grad_norm, axis=-1, keepdims=True)
    second_mean = jnp.mean(grad_norm * unit_norm, axis=-1, keepdims=True)
    return inv_std * (grad_norm - first_mean - unit_norm * second_mean)


def partner(values, bit):
    count = lax.axis_size("dp")
    return lax.ppermute(values, "dp", [(i, i ^ bit) for i in range(count)])


def other_row(values):
    return lax.ppermute(values, "rows", [(0, 1), (1, 0)])


def pick(values, which, axis):
    return lax.dynamic_index_in_dim(values, which, axis, keepdims=False)


def halved_dp(slices, bits, bit):
    at = bits.index(bit)
    low = 1 << (len(bits) - 1 - at)
    grouped = slices.reshape((slices.shape[0] // (2 * low), 2, low) + slices.shape[1:])
    mine = (lax.axis_index("dp") // bit) % 2
    sent = pick(grouped, 1 - mine, 1).astype(jnp.bfloat16)
    total = pick(grouped, mine, 1) + partner(sent, bit).astype(jnp.float32)
    return total.reshape((slices.shape[0] // 2,) + slices.shape[1:]), [b for b in bits if b != bit]


def halved_rows(slices):
    half = slices.shape[-1] // 2
    mine = lax.axis_index("rows")
    sent = lax.dynamic_slice_in_dim(slices, (1 - mine) * half, half, axis=2).astype(jnp.bfloat16)
    kept = lax.dynamic_slice_in_dim(slices, mine * half, half, axis=2)
    return kept + other_row(sent).astype(jnp.float32)


def joined_rows(half):
    sent = half.astype(jnp.bfloat16)
    other = other_row(sent)
    first = lax.axis_index("rows") == 0
    return jnp.concatenate(
        [jnp.where(first, sent, other), jnp.where(first, other, sent)], axis=-1
    ).astype(jnp.float32)


def scattered(partial, order):
    count = lax.axis_size("dp")
    slices = partial.reshape(count, partial.shape[0] // count, partial.shape[1])
    bits = [1 << k for k in reversed(range(count.bit_length() - 1))]
    for stage in order:
        if stage == "rows":
            slices = halved_rows(slices)
        else:
            slices, bits = halved_dp(slices, bits, stage)
    return joined_rows(slices[0])


def summed_everywhere(values):
    count = lax.axis_size("dp")
    bit = 1
    while bit < count:
        values = values + partner(values, bit)
        bit *= 2
    return values + other_row(values)


def pointwise(tokens, cot_rows, up_full, down_full):
    pre_act = jnp.dot(tokens, up_full, preferred_element_type=jnp.float32)
    hidden, derivative = gelu_parts(pre_act)
    activation = hidden.astype(jnp.bfloat16)
    branch = jnp.dot(activation, down_full, preferred_element_type=jnp.float32)
    grad_act = lax.dot_general(
        cot_rows, down_full, (((1,), (1,)), ((), ())), preferred_element_type=jnp.float32
    )
    grad_pre = (grad_act * derivative).astype(jnp.bfloat16)
    grad_norm = lax.dot_general(
        grad_pre, up_full, (((1,), (1,)), ((), ())), preferred_element_type=jnp.float32
    )
    return (activation, branch, grad_pre, grad_norm)


def on_device(features, bucket, kernel, up_weight, down_weight, cotangent):
    images, strip_rows, canvas_cols, channels = features.shape
    rows_count = lax.axis_size("rows")
    row_index = lax.axis_index("rows")
    canvas_rows = strip_rows * rows_count
    area_cells = canvas_rows * canvas_cols // 2
    reach = kernel.shape[0] // 2
    grad_scale = 1.0 / (images * lax.axis_size("dp"))
    heights = canvas_rows // 2 + bucket
    widths = jnp.minimum(canvas_cols, area_cells // heights)
    row_ids = row_index * strip_rows + lax.iota(jnp.int32, strip_rows)
    col_ids = lax.iota(jnp.int32, canvas_cols)
    inside = (row_ids[None, :, None] < heights[:, None, None]) & (
        col_ids[None, None, :] < widths[:, None, None]
    )
    inside_cells = inside[..., None]
    masked = jnp.where(inside_cells, features, jnp.zeros((), features.dtype))
    masked_cot = jnp.where(inside_cells, cotangent, jnp.zeros((), cotangent.dtype))
    up_full, down_full = (
        lax.all_gather(up_weight, "dp", axis=0, tiled=True),
        lax.all_gather(down_weight, "dp", axis=0, tiled=True),
    )
    rimmed = padded_2(masked, (("rows", 1),), reach)
    padded = jnp.pad(rimmed, ((0, 0), (0, 0), (reach, reach), (0, 0)))
    convolved = jnp.where(
        inside_cells, depthwise(padded, kernel, strip_rows, canvas_cols, False), 0.0
    )
    unit_norm, inv_std = layer_norm(convolved)
    normed = unit_norm.astype(jnp.bfloat16)
    tokens = normed.reshape(images * strip_rows * canvas_cols, channels)
    cot_rows = masked_cot.reshape(images * strip_rows * canvas_cols, channels)
    activation, branch_rows, grad_pre, grad_rows = pointwise(tokens, cot_rows, up_full, down_full)
    branch = branch_rows.reshape(features.shape)
    grad_norm = grad_rows.reshape(features.shape)
    block_out = (masked + branch).astype(jnp.bfloat16)
    grad_conv = jnp.where(inside_cells, norm_backward(grad_norm, unit_norm, inv_std), 0.0)
    kernel_grad = summed_everywhere(
        kernel_terms(grad_conv, padded, kernel.shape[0]) * grad_scale
    )
    grad_rimmed = padded_2(grad_conv.astype(jnp.bfloat16), (("rows", 1),), reach).astype(
        grad_conv.dtype
    )
    grad_padded = jnp.pad(grad_rimmed, ((0, 0), (0, 0), (reach, reach), (0, 0)))
    feature_grad = jnp.where(
        inside_cells,
        masked_cot + depthwise(grad_padded, kernel, strip_rows, canvas_cols, True),
        0.0,
    ).astype(jnp.bfloat16)
    dp_bits = [1 << k for k in range(lax.axis_size("dp").bit_length() - 1)]
    down_grad = scattered(
        lax.dot_general(
            activation, cot_rows, (((0,), (0,)), ((), ())), preferred_element_type=jnp.float32
        )
        * grad_scale,
        dp_bits + ["rows"],
    )
    up_grad = scattered(
        lax.dot_general(
            tokens, grad_pre, (((0,), (0,)), ((), ())), preferred_element_type=jnp.float32
        )
        * grad_scale,
        dp_bits[:1] + ["rows"] + dp_bits[2:] + dp_bits[1:2],
    )
    return (block_out, feature_grad, up_grad, down_grad, kernel_grad)


def solution(mesh):
    placed = (
        P("dp", "rows", None, None),
        P("dp"),
        P(),
        P("dp", None),
        P("dp", None),
        P("dp", "rows", None, None),
    )
    return jax.shard_map(
        on_device,
        mesh=mesh,
        in_specs=placed,
        out_specs=(
            P("dp", "rows", None, None),
            P("dp", "rows", None, None),
            P("dp", None),
            P("dp", None),
            P(),
        ),
        check_vma=False,
    )
```

```python
import jax
import jax.numpy as jnp
from jax import lax
from jax.sharding import PartitionSpec as P

INV_ROOT_TWO = 0.7071067811865476
INV_ROOT_TAU = 0.3989422804014327
EPSILON = 1e-06


def padded_2(block, sides, width):
    for axis, dim in sides:
        count = lax.axis_size(axis)
        forward = [(i, i + 1) for i in range(count - 1)]
        backward = [(target, source) for source, target in forward]
        low = lax.ppermute(
            lax.slice_in_dim(block, block.shape[dim] - width, None, axis=dim), axis, forward
        )
        high = lax.ppermute(lax.slice_in_dim(block, 0, width, axis=dim), axis, backward)
        block = jnp.concatenate([low, block, high], axis=dim)
    return block


def gelu_parts(pre_act):
    normal_cdf = 0.5 * (1.0 + lax.erf(pre_act * INV_ROOT_TWO))
    density = jnp.exp(-0.5 * pre_act * pre_act) * INV_ROOT_TAU
    return (pre_act * normal_cdf, normal_cdf + pre_act * density)


def depthwise(padded, kernel, out_rows, out_cols, flipped):
    span = kernel.shape[0]
    result = jnp.zeros(padded.shape[:-3] + (out_rows, out_cols, padded.shape[-1]), jnp.float32)
    for offset_row in range(span):
        for offset_col in range(span):
            start_row = span - 1 - offset_row if flipped else offset_row
            start_col = span - 1 - offset_col if flipped else offset_col
            result = (
                result
                + kernel[offset_row, offset_col]
                * padded[..., start_row : start_row + out_rows, start_col : start_col + out_cols, :]
            )
    return result


def kernel_terms(grad_conv, padded, span):
    reduce_axes = tuple(range(grad_conv.ndim - 1))
    rows_out = grad_conv.shape[-3]
    cols_out = grad_conv.shape[-2]
    kernel_rows = []
    for offset_row in range(span):
        kernel_row = []
        for offset_col in range(span):
            window = padded[
                ..., offset_row : offset_row + rows_out, offset_col : offset_col + cols_out, :
            ]
            kernel_row.append(jnp.sum(grad_conv * window, axis=reduce_axes))
        kernel_rows.append(jnp.stack(kernel_row))
    return jnp.stack(kernel_rows)


def layer_norm(convolved):
    centered = convolved - jnp.mean(convolved, axis=-1, keepdims=True)
    inv_std = lax.rsqrt(jnp.mean(centered * centered, axis=-1, keepdims=True) + EPSILON)
    return (centered * inv_std, inv_std)


def norm_backward(grad_norm, unit_norm, inv_std):
    first_mean = jnp.mean(grad_norm, axis=-1, keepdims=True)
    second_mean = jnp.mean(grad_norm * unit_norm, axis=-1, keepdims=True)
    return inv_std * (grad_norm - first_mean - unit_norm * second_mean)


def partner(values, bit):
    count = lax.axis_size("dp")
    return lax.ppermute(values, "dp", [(i, i ^ bit) for i in range(count)])


def other_row(values):
    return lax.ppermute(values, "rows", [(0, 1), (1, 0)])


def pick(values, which, axis):
    return lax.dynamic_index_in_dim(values, which, axis, keepdims=False)


def place():
    index = lax.axis_index("dp")
    return index // 4, (index // 2) % 2, index % 2


def halved_dp(slices, axis, mine, bit):
    sent = pick(slices, 1 - mine, axis).astype(jnp.bfloat16)
    return pick(slices, mine, axis) + partner(sent, bit).astype(jnp.float32)


def halved_rows(slices):
    half = slices.shape[-1] // 2
    axis = slices.ndim - 1
    mine = lax.axis_index("rows")
    sent = lax.dynamic_slice_in_dim(slices, (1 - mine) * half, half, axis=axis)
    kept = lax.dynamic_slice_in_dim(slices, mine * half, half, axis=axis)
    return kept + other_row(sent.astype(jnp.bfloat16)).astype(jnp.float32)


def in_order(mine, own, other, axis, stacked):
    first = mine == 0
    pair = [jnp.where(first, own, other), jnp.where(first, other, own)]
    return jnp.stack(pair, axis=axis) if stacked else jnp.concatenate(pair, axis=axis)


def both_rows(half):
    return in_order(lax.axis_index("rows"), half, other_row(half), half.ndim - 1, False)


def scatter_core(partial):
    line = lax.axis_size("dp") // 4
    slices = partial.reshape(line, 2, 2, partial.shape[0] // (4 * line), partial.shape[1])
    return halved_dp(slices, 2, place()[2], 1)


def scatter_first(slices):
    cut = slices.shape[0] // 2
    return halved_rows(slices[:cut]), halved_dp(slices[cut:], 1, place()[1], 2)


def scatter_second(low, high):
    return jnp.concatenate([halved_dp(low, 1, place()[1], 2), halved_rows(high)], axis=0)


def scatter_line(slices):
    at = place()[0]
    total = pick(slices, at, 0)
    for step in range(1, slices.shape[0]):
        sent = pick(slices, at ^ step, 0).astype(jnp.bfloat16)
        total = total + partner(sent, 4 * step).astype(jnp.float32)
    return total


def scatter_last(half):
    return both_rows(half.astype(jnp.bfloat16)).astype(jnp.float32)


def gathered(weight):
    line = lax.axis_size("dp") // 4
    at, middle, core = place()
    half = weight.shape[1] // 2
    own = lax.dynamic_slice_in_dim(weight, lax.axis_index("rows") * half, half, axis=1)
    pieces = [own] + [partner(own, 4 * step) for step in range(1, line)]
    bit = 1
    while bit < line:
        swap = (at // bit) % 2 == 1
        pieces = [jnp.where(swap, pieces[j ^ bit], pieces[j]) for j in range(line)]
        bit *= 2
    low, high = jnp.stack(pieces[: line // 2]), jnp.stack(pieces[line // 2 :])
    low = in_order(middle, low, partner(low, 2), 1, True)
    high = both_rows(high)
    low = both_rows(low)
    high = in_order(middle, high, partner(high, 2), 1, True)
    slices = jnp.concatenate([low, high], axis=0)
    slices = in_order(core, slices, partner(slices, 1), 2, True)
    return slices.reshape(weight.shape[0] * 4 * line, weight.shape[1])


def summed_everywhere(values):
    count = lax.axis_size("dp")
    bit = 1
    while bit < count:
        values = values + partner(values, bit)
        bit *= 2
    return values + other_row(values)


def on_device(features, bucket, kernel, up_weight, down_weight, cotangent):
    images, strip_rows, canvas_cols, channels = features.shape
    rows_count = lax.axis_size("rows")
    row_index = lax.axis_index("rows")
    canvas_rows = strip_rows * rows_count
    area_cells = canvas_rows * canvas_cols // 2
    reach = kernel.shape[0] // 2
    grad_scale = 1.0 / (images * lax.axis_size("dp"))
    heights = canvas_rows // 2 + bucket
    widths = jnp.minimum(canvas_cols, area_cells // heights)
    row_ids = row_index * strip_rows + lax.iota(jnp.int32, strip_rows)
    col_ids = lax.iota(jnp.int32, canvas_cols)
    inside = (row_ids[None, :, None] < heights[:, None, None]) & (
        col_ids[None, None, :] < widths[:, None, None]
    )
    inside_cells = inside[..., None]
    masked = jnp.where(inside_cells, features, jnp.zeros((), features.dtype))
    masked_cot = jnp.where(inside_cells, cotangent, jnp.zeros((), cotangent.dtype))
    up_full, down_full = (
        gathered(up_weight),
        lax.all_gather(down_weight, "dp", axis=0, tiled=True),
    )
    rimmed = padded_2(masked, (("rows", 1),), reach)
    padded = jnp.pad(rimmed, ((0, 0), (0, 0), (reach, reach), (0, 0)))
    convolved = jnp.where(
        inside_cells, depthwise(padded, kernel, strip_rows, canvas_cols, False), 0.0
    )
    unit_norm, inv_std = layer_norm(convolved)
    normed = unit_norm.astype(jnp.bfloat16)
    tokens = normed.reshape(images * strip_rows * canvas_cols, channels)
    cot_rows = masked_cot.reshape(images * strip_rows * canvas_cols, channels)
    pre_act = jnp.dot(tokens, up_full, preferred_element_type=jnp.float32)
    hidden, derivative = gelu_parts(pre_act)
    activation = hidden.astype(jnp.bfloat16)
    down_part = (
        lax.dot_general(
            activation, cot_rows, (((0,), (0,)), ((), ())), preferred_element_type=jnp.float32
        )
        * grad_scale
    )
    down_part = scatter_core(down_part)
    down_full, down_part = lax.optimization_barrier((down_full, down_part))
    down_low, down_high = scatter_first(down_part)
    grad_act = lax.dot_general(
        cot_rows, down_full, (((1,), (1,)), ((), ())), preferred_element_type=jnp.float32
    )
    grad_pre = (grad_act * derivative).astype(jnp.bfloat16)
    up_part = (
        lax.dot_general(
            tokens, grad_pre, (((0,), (0,)), ((), ())), preferred_element_type=jnp.float32
        )
        * grad_scale
    )
    up_part = scatter_core(up_part)
    grad_rows = lax.dot_general(
        grad_pre, up_full, (((1,), (1,)), ((), ())), preferred_element_type=jnp.float32
    )
    grad_norm = grad_rows.reshape(features.shape)
    grad_conv = jnp.where(inside_cells, norm_backward(grad_norm, unit_norm, inv_std), 0.0)
    grad_conv, up_part, down_low, down_high = lax.optimization_barrier(
        (grad_conv, up_part, down_low, down_high)
    )
    down_part = scatter_second(down_low, down_high)
    up_low, up_high = scatter_first(up_part)
    grad_rimmed = padded_2(grad_conv.astype(jnp.bfloat16), (("rows", 1),), reach).astype(
        grad_conv.dtype
    )
    kernel_part = kernel_terms(grad_conv, padded, kernel.shape[0]) * grad_scale
    kernel_part, grad_rimmed, down_part, up_low, up_high = lax.optimization_barrier(
        (kernel_part, grad_rimmed, down_part, up_low, up_high)
    )
    kernel_grad = summed_everywhere(kernel_part)
    down_half = scatter_line(down_part)
    up_part = scatter_second(up_low, up_high)
    grad_padded = jnp.pad(grad_rimmed, ((0, 0), (0, 0), (reach, reach), (0, 0)))
    feature_grad = jnp.where(
        inside_cells,
        masked_cot + depthwise(grad_padded, kernel, strip_rows, canvas_cols, True),
        0.0,
    ).astype(jnp.bfloat16)
    feature_grad, activation, down_half, up_part = lax.optimization_barrier(
        (feature_grad, activation, down_half, up_part)
    )
    up_half = scatter_line(up_part)
    branch = jnp.dot(activation, down_full, preferred_element_type=jnp.float32)
    block_out = (masked + branch.reshape(features.shape)).astype(jnp.bfloat16)
    down_grad = scatter_last(down_half)
    up_grad = scatter_last(up_half)
    return (block_out, feature_grad, up_grad, down_grad, kernel_grad)


def solution(mesh):
    placed = (
        P("dp", "rows", None, None),
        P("dp"),
        P(),
        P("dp", None),
        P("dp", None),
        P("dp", "rows", None, None),
    )
    return jax.shard_map(
        on_device,
        mesh=mesh,
        in_specs=placed,
        out_specs=(
            P("dp", "rows", None, None),
            P("dp", "rows", None, None),
            P("dp", None),
            P("dp", None),
            P(),
        ),
        check_vma=False,
    )
```

```python
import functools

import jax
import jax.numpy as jnp
from jax import lax
from jax.experimental import pallas as pl
from jax.experimental.pallas import tpu as pltpu
from jax.sharding import PartitionSpec as P

INV_ROOT_TWO = 0.7071067811865476
INV_ROOT_TAU = 0.3989422804014327
EPSILON = 1e-06


def padded_2(block, sides, width):
    for axis, dim in sides:
        count = lax.axis_size(axis)
        forward = [(i, i + 1) for i in range(count - 1)]
        backward = [(target, source) for source, target in forward]
        low = lax.ppermute(
            lax.slice_in_dim(block, block.shape[dim] - width, None, axis=dim), axis, forward
        )
        high = lax.ppermute(lax.slice_in_dim(block, 0, width, axis=dim), axis, backward)
        block = jnp.concatenate([low, block, high], axis=dim)
    return block


def gelu_parts(pre_act):
    normal_cdf = 0.5 * (1.0 + lax.erf(pre_act * INV_ROOT_TWO))
    density = jnp.exp(-0.5 * pre_act * pre_act) * INV_ROOT_TAU
    return (pre_act * normal_cdf, normal_cdf + pre_act * density)


LANES = 128
SUBLANES = 8


def depthwise_kernel(flipped, padded_ref, kernel_ref, out_ref):
    span = kernel_ref.shape[0]
    rows, cols = out_ref.shape[1], out_ref.shape[2]
    for col in range(0, cols, SUBLANES):
        sums = [jnp.zeros((SUBLANES, LANES), jnp.float32)] * rows
        for start_col in range(span):
            offset_col = span - 1 - start_col if flipped else start_col
            taps = [
                jnp.broadcast_to(
                    kernel_ref[span - 1 - a if flipped else a, pl.ds(offset_col, 1), :],
                    (SUBLANES, LANES),
                )
                for a in range(span)
            ]
            for source in range(rows + span - 1):
                window = padded_ref[0, source, pl.ds(col + start_col, SUBLANES), :]
                for a in range(span):
                    if 0 <= source - a < rows:
                        sums[source - a] = sums[source - a] + taps[a] * window
        for row in range(rows):
            out_ref[0, row, pl.ds(col, SUBLANES), :] = sums[row]


def depthwise(padded, kernel, out_rows, out_cols, flipped):
    images, channels = padded.shape[0], padded.shape[-1]
    span = kernel.shape[0]
    taps = span * span * out_rows * out_cols * channels * images
    return pl.pallas_call(
        functools.partial(depthwise_kernel, flipped),
        grid=(images, channels // LANES),
        in_specs=[
            pl.BlockSpec((1,) + padded.shape[1:3] + (LANES,), lambda i, c: (i, 0, 0, c)),
            pl.BlockSpec((span, span, LANES), lambda i, c: (0, 0, c)),
        ],
        out_specs=pl.BlockSpec((1, out_rows, out_cols, LANES), lambda i, c: (i, 0, 0, c)),
        out_shape=jax.ShapeDtypeStruct((images, out_rows, out_cols, channels), jnp.float32),
        cost_estimate=pl.CostEstimate(
            flops=2 * taps, bytes_accessed=4 * padded.size, transcendentals=0
        ),
        compiler_params=pltpu.CompilerParams(vmem_limit_bytes=16 * 1024 * 1024),
    )(padded.astype(jnp.float32), kernel)


def kernel_terms_kernel(span, grad_ref, padded_ref, out_ref):
    rows, cols = grad_ref.shape[1], grad_ref.shape[2]
    for col in range(0, cols, SUBLANES):
        grads = [grad_ref[0, row, pl.ds(col, SUBLANES), :] for row in range(rows)]
        for offset_col in range(span):
            sums = [jnp.zeros((SUBLANES, LANES), jnp.float32)] * span
            for source in range(rows + span - 1):
                window = padded_ref[0, source, pl.ds(col + offset_col, SUBLANES), :]
                for a in range(span):
                    if 0 <= source - a < rows:
                        sums[a] = sums[a] + grads[source - a] * window
            for a in range(span):
                if col == 0:
                    out_ref[0, a * span + offset_col] = sums[a]
                else:
                    out_ref[0, a * span + offset_col] += sums[a]


def kernel_terms(grad_conv, padded, span):
    images, rows, cols, channels = grad_conv.shape
    taps = span * span * grad_conv.size
    terms = pl.pallas_call(
        functools.partial(kernel_terms_kernel, span),
        grid=(images, channels // LANES),
        in_specs=[
            pl.BlockSpec((1, rows, cols, LANES), lambda i, c: (i, 0, 0, c)),
            pl.BlockSpec((1,) + padded.shape[1:3] + (LANES,), lambda i, c: (i, 0, 0, c)),
        ],
        out_specs=pl.BlockSpec((1, span * span, SUBLANES, LANES), lambda i, c: (i, 0, 0, c)),
        out_shape=jax.ShapeDtypeStruct((images, span * span, SUBLANES, channels), jnp.float32),
        cost_estimate=pl.CostEstimate(
            flops=2 * taps, bytes_accessed=4 * padded.size, transcendentals=0
        ),
        compiler_params=pltpu.CompilerParams(vmem_limit_bytes=16 * 1024 * 1024),
    )(grad_conv, padded.astype(jnp.float32))
    return jnp.sum(terms, axis=(0, 2)).reshape(span, span, channels)


def layer_norm(convolved):
    centered = convolved - jnp.mean(convolved, axis=-1, keepdims=True)
    inv_std = lax.rsqrt(jnp.mean(centered * centered, axis=-1, keepdims=True) + EPSILON)
    return (centered * inv_std, inv_std)


def norm_backward(grad_norm, unit_norm, inv_std):
    first_mean = jnp.mean(grad_norm, axis=-1, keepdims=True)
    second_mean = jnp.mean(grad_norm * unit_norm, axis=-1, keepdims=True)
    return inv_std * (grad_norm - first_mean - unit_norm * second_mean)


def partner(values, bit):
    count = lax.axis_size("dp")
    return lax.ppermute(values, "dp", [(i, i ^ bit) for i in range(count)])


def other_row(values):
    return lax.ppermute(values, "rows", [(0, 1), (1, 0)])


def pick(values, which, axis):
    return lax.dynamic_index_in_dim(values, which, axis, keepdims=False)


def place():
    index = lax.axis_index("dp")
    return index // 4, (index // 2) % 2, index % 2


def halved_dp(slices, axis, mine, bit):
    sent = pick(slices, 1 - mine, axis).astype(jnp.bfloat16)
    return pick(slices, mine, axis) + partner(sent, bit).astype(jnp.float32)


def halved_rows(slices):
    half = slices.shape[-1] // 2
    axis = slices.ndim - 1
    mine = lax.axis_index("rows")
    sent = lax.dynamic_slice_in_dim(slices, (1 - mine) * half, half, axis=axis)
    kept = lax.dynamic_slice_in_dim(slices, mine * half, half, axis=axis)
    return kept + other_row(sent.astype(jnp.bfloat16)).astype(jnp.float32)


def in_order(mine, own, other, axis, stacked):
    first = mine == 0
    pair = [jnp.where(first, own, other), jnp.where(first, other, own)]
    return jnp.stack(pair, axis=axis) if stacked else jnp.concatenate(pair, axis=axis)


def both_rows(half):
    return in_order(lax.axis_index("rows"), half, other_row(half), half.ndim - 1, False)


def scatter_core(partial):
    line = lax.axis_size("dp") // 4
    slices = partial.reshape(line, 2, 2, partial.shape[0] // (4 * line), partial.shape[1])
    return halved_dp(slices, 2, place()[2], 1)


def scatter_first(slices):
    cut = slices.shape[0] // 2
    return halved_rows(slices[:cut]), halved_dp(slices[cut:], 1, place()[1], 2)


def scatter_second(low, high):
    return jnp.concatenate([halved_dp(low, 1, place()[1], 2), halved_rows(high)], axis=0)


def scatter_line(slices):
    at = place()[0]
    total = pick(slices, at, 0)
    for step in range(1, slices.shape[0]):
        sent = pick(slices, at ^ step, 0).astype(jnp.bfloat16)
        total = total + partner(sent, 4 * step).astype(jnp.float32)
    return total


def scatter_last(half):
    return both_rows(half.astype(jnp.bfloat16)).astype(jnp.float32)


def gather_line(weight):
    line = lax.axis_size("dp") // 4
    at = place()[0]
    half = weight.shape[1] // 2
    own = lax.dynamic_slice_in_dim(weight, lax.axis_index("rows") * half, half, axis=1)
    pieces = [own] + [partner(own, 4 * step) for step in range(1, line)]
    bit = 1
    while bit < line:
        swap = (at // bit) % 2 == 1
        pieces = [jnp.where(swap, pieces[j ^ bit], pieces[j]) for j in range(line)]
        bit *= 2
    return jnp.stack(pieces[: line // 2]), jnp.stack(pieces[line // 2 :])


def gather_middle(slices):
    return in_order(place()[1], slices, partner(slices, 2), 1, True)


def gather_core(low, high):
    slices = jnp.concatenate([low, high], axis=0)
    slices = in_order(place()[2], slices, partner(slices, 1), 2, True)
    return slices.reshape(-1, slices.shape[-1])


def summed_line(values):
    line = lax.axis_size("dp") // 4
    at = place()[0]
    pieces = [values] + [partner(values, 4 * step) for step in range(1, line)]
    bit = 1
    while bit < line:
        swap = (at // bit) % 2 == 1
        pieces = [jnp.where(swap, pieces[j ^ bit], pieces[j]) for j in range(line)]
        bit *= 2
    return functools.reduce(jnp.add, pieces)


def on_device(features, bucket, kernel, up_weight, down_weight, cotangent):
    images, strip_rows, canvas_cols, channels = features.shape
    rows_count = lax.axis_size("rows")
    row_index = lax.axis_index("rows")
    canvas_rows = strip_rows * rows_count
    area_cells = canvas_rows * canvas_cols // 2
    reach = kernel.shape[0] // 2
    grad_scale = 1.0 / (images * lax.axis_size("dp"))
    heights = canvas_rows // 2 + bucket
    widths = jnp.minimum(canvas_cols, area_cells // heights)
    row_ids = row_index * strip_rows + lax.iota(jnp.int32, strip_rows)
    col_ids = lax.iota(jnp.int32, canvas_cols)
    inside = (row_ids[None, :, None] < heights[:, None, None]) & (
        col_ids[None, None, :] < widths[:, None, None]
    )
    inside_cells = inside[..., None]
    masked = jnp.where(inside_cells, features, jnp.zeros((), features.dtype))
    masked_cot = jnp.where(inside_cells, cotangent, jnp.zeros((), cotangent.dtype))
    down_full = lax.all_gather(down_weight, "dp", axis=0, tiled=True)
    up_low, up_high = gather_line(up_weight)
    rimmed = padded_2(masked, (("rows", 1),), reach)
    padded = jnp.pad(rimmed, ((0, 0), (0, 0), (reach, reach), (0, 0))).astype(jnp.float32)
    padded, up_low, up_high = lax.optimization_barrier((padded, up_low, up_high))
    up_low, up_high = gather_middle(up_low), both_rows(up_high)
    convolved = depthwise(padded, kernel, strip_rows, canvas_cols, False)
    convolved, up_low, up_high = lax.optimization_barrier((convolved, up_low, up_high))
    up_low, up_high = both_rows(up_low), gather_middle(up_high)
    convolved = jnp.where(inside_cells, convolved, 0.0)
    unit_norm, inv_std = layer_norm(convolved)
    normed = unit_norm.astype(jnp.bfloat16)
    tokens = normed.reshape(images * strip_rows * canvas_cols, channels)
    cot_rows = masked_cot.reshape(images * strip_rows * canvas_cols, channels)
    up_full = gather_core(up_low, up_high)
    pre_act = jnp.dot(tokens, up_full, preferred_element_type=jnp.float32)
    hidden, derivative = gelu_parts(pre_act)
    activation = hidden.astype(jnp.bfloat16)
    down_part = (
        lax.dot_general(
            activation, cot_rows, (((0,), (0,)), ((), ())), preferred_element_type=jnp.float32
        )
        * grad_scale
    )
    down_part = scatter_core(down_part)
    down_full, down_part = lax.optimization_barrier((down_full, down_part))
    down_low, down_high = scatter_first(down_part)
    grad_act = lax.dot_general(
        cot_rows, down_full, (((1,), (1,)), ((), ())), preferred_element_type=jnp.float32
    )
    grad_pre = (grad_act * derivative).astype(jnp.bfloat16)
    up_part = (
        lax.dot_general(
            tokens, grad_pre, (((0,), (0,)), ((), ())), preferred_element_type=jnp.float32
        )
        * grad_scale
    )
    up_part = scatter_core(up_part)
    grad_rows = lax.dot_general(
        grad_pre, up_full, (((1,), (1,)), ((), ())), preferred_element_type=jnp.float32
    )
    grad_norm = grad_rows.reshape(features.shape)
    grad_conv = jnp.where(inside_cells, norm_backward(grad_norm, unit_norm, inv_std), 0.0)
    grad_conv, up_part, down_low, down_high = lax.optimization_barrier(
        (grad_conv, up_part, down_low, down_high)
    )
    down_part = scatter_second(down_low, down_high)
    up_low, up_high = scatter_first(up_part)
    grad_rimmed = padded_2(grad_conv.astype(jnp.bfloat16), (("rows", 1),), reach).astype(
        grad_conv.dtype
    )
    kernel_part = kernel_terms(grad_conv, padded, kernel.shape[0]) * grad_scale
    kernel_part, grad_rimmed, down_part, up_low, up_high = lax.optimization_barrier(
        (kernel_part, grad_rimmed, down_part, up_low, up_high)
    )
    kernel_part = kernel_part + partner(kernel_part, 1)
    down_half = scatter_line(down_part)
    up_part = scatter_second(up_low, up_high)
    grad_padded = jnp.pad(grad_rimmed, ((0, 0), (0, 0), (reach, reach), (0, 0)))
    feature_grad = jnp.where(
        inside_cells,
        masked_cot + depthwise(grad_padded, kernel, strip_rows, canvas_cols, True),
        0.0,
    ).astype(jnp.bfloat16)
    feature_grad, activation, down_half, up_part, kernel_part = lax.optimization_barrier(
        (feature_grad, activation, down_half, up_part, kernel_part)
    )
    kernel_part = kernel_part + partner(kernel_part, 2)
    up_half = scatter_line(up_part)
    branch = jnp.dot(activation, down_full, preferred_element_type=jnp.float32)
    block_out = (masked + branch.reshape(features.shape)).astype(jnp.bfloat16)
    kernel_grad = summed_line(kernel_part + other_row(kernel_part))
    down_grad = scatter_last(down_half)
    up_grad = scatter_last(up_half)
    return (block_out, feature_grad, up_grad, down_grad, kernel_grad)


def solution(mesh):
    placed = (
        P("dp", "rows", None, None),
        P("dp"),
        P(),
        P("dp", None),
        P("dp", None),
        P("dp", "rows", None, None),
    )
    return jax.shard_map(
        on_device,
        mesh=mesh,
        in_specs=placed,
        out_specs=(
            P("dp", "rows", None, None),
            P("dp", "rows", None, None),
            P("dp", None),
            P("dp", None),
            P(),
        ),
        check_vma=False,
    )
```

```python
import functools

import jax
import jax.numpy as jnp
from jax import lax
from jax.experimental import pallas as pl
from jax.experimental.pallas import tpu as pltpu
from jax.sharding import PartitionSpec as P

INV_ROOT_TWO = 0.7071067811865476
INV_ROOT_TAU = 0.3989422804014327
EPSILON = 1e-06


def padded_2(block, sides, width):
    for axis, dim in sides:
        count = lax.axis_size(axis)
        forward = [(i, i + 1) for i in range(count - 1)]
        backward = [(target, source) for source, target in forward]
        low = lax.ppermute(
            lax.slice_in_dim(block, block.shape[dim] - width, None, axis=dim), axis, forward
        )
        high = lax.ppermute(lax.slice_in_dim(block, 0, width, axis=dim), axis, backward)
        block = jnp.concatenate([low, block, high], axis=dim)
    return block


def gelu_parts(pre_act):
    normal_cdf = 0.5 * (1.0 + lax.erf(pre_act * INV_ROOT_TWO))
    density = jnp.exp(-0.5 * pre_act * pre_act) * INV_ROOT_TAU
    return (pre_act * normal_cdf, normal_cdf + pre_act * density)


LANES = 128
SUBLANES = 8


def depthwise_kernel(flipped, padded_ref, kernel_ref, out_ref):
    span = kernel_ref.shape[0]
    rows, cols = out_ref.shape[1], out_ref.shape[2]
    for col in range(0, cols, SUBLANES):
        sums = [jnp.zeros((SUBLANES, LANES), jnp.float32)] * rows
        for start_col in range(span):
            offset_col = span - 1 - start_col if flipped else start_col
            taps = [
                jnp.broadcast_to(
                    kernel_ref[span - 1 - a if flipped else a, pl.ds(offset_col, 1), :],
                    (SUBLANES, LANES),
                )
                for a in range(span)
            ]
            for source in range(rows + span - 1):
                window = padded_ref[0, source, pl.ds(col + start_col, SUBLANES), :]
                for a in range(span):
                    if 0 <= source - a < rows:
                        sums[source - a] = sums[source - a] + taps[a] * window
        for row in range(rows):
            out_ref[0, row, pl.ds(col, SUBLANES), :] = sums[row]


def depthwise(padded, kernel, out_rows, out_cols, flipped):
    images, channels = padded.shape[0], padded.shape[-1]
    span = kernel.shape[0]
    taps = span * span * out_rows * out_cols * channels * images
    return pl.pallas_call(
        functools.partial(depthwise_kernel, flipped),
        grid=(images, channels // LANES),
        in_specs=[
            pl.BlockSpec((1,) + padded.shape[1:3] + (LANES,), lambda i, c: (i, 0, 0, c)),
            pl.BlockSpec((span, span, LANES), lambda i, c: (0, 0, c)),
        ],
        out_specs=pl.BlockSpec((1, out_rows, out_cols, LANES), lambda i, c: (i, 0, 0, c)),
        out_shape=jax.ShapeDtypeStruct((images, out_rows, out_cols, channels), jnp.float32),
        cost_estimate=pl.CostEstimate(
            flops=2 * taps, bytes_accessed=4 * padded.size, transcendentals=0
        ),
        compiler_params=pltpu.CompilerParams(vmem_limit_bytes=16 * 1024 * 1024),
    )(padded.astype(jnp.float32), kernel)


def kernel_terms_kernel(span, grad_ref, padded_ref, out_ref):
    rows, cols = grad_ref.shape[1], grad_ref.shape[2]
    for col in range(0, cols, SUBLANES):
        grads = [grad_ref[0, row, pl.ds(col, SUBLANES), :] for row in range(rows)]
        for offset_col in range(span):
            sums = [jnp.zeros((SUBLANES, LANES), jnp.float32)] * span
            for source in range(rows + span - 1):
                window = padded_ref[0, source, pl.ds(col + offset_col, SUBLANES), :]
                for a in range(span):
                    if 0 <= source - a < rows:
                        sums[a] = sums[a] + grads[source - a] * window
            for a in range(span):
                if col == 0:
                    out_ref[0, a * span + offset_col] = sums[a]
                else:
                    out_ref[0, a * span + offset_col] += sums[a]


def kernel_terms(grad_conv, padded, span):
    images, rows, cols, channels = grad_conv.shape
    taps = span * span * grad_conv.size
    terms = pl.pallas_call(
        functools.partial(kernel_terms_kernel, span),
        grid=(images, channels // LANES),
        in_specs=[
            pl.BlockSpec((1, rows, cols, LANES), lambda i, c: (i, 0, 0, c)),
            pl.BlockSpec((1,) + padded.shape[1:3] + (LANES,), lambda i, c: (i, 0, 0, c)),
        ],
        out_specs=pl.BlockSpec((1, span * span, SUBLANES, LANES), lambda i, c: (i, 0, 0, c)),
        out_shape=jax.ShapeDtypeStruct((images, span * span, SUBLANES, channels), jnp.float32),
        cost_estimate=pl.CostEstimate(
            flops=2 * taps, bytes_accessed=4 * padded.size, transcendentals=0
        ),
        compiler_params=pltpu.CompilerParams(vmem_limit_bytes=16 * 1024 * 1024),
    )(grad_conv, padded.astype(jnp.float32))
    return jnp.sum(terms, axis=(0, 2)).reshape(span, span, channels)


def layer_norm(convolved):
    centered = convolved - jnp.mean(convolved, axis=-1, keepdims=True)
    inv_std = lax.rsqrt(jnp.mean(centered * centered, axis=-1, keepdims=True) + EPSILON)
    return (centered * inv_std, inv_std)


def norm_backward(grad_norm, unit_norm, inv_std):
    first_mean = jnp.mean(grad_norm, axis=-1, keepdims=True)
    second_mean = jnp.mean(grad_norm * unit_norm, axis=-1, keepdims=True)
    return inv_std * (grad_norm - first_mean - unit_norm * second_mean)


def partner(values, bit):
    count = lax.axis_size("dp")
    return lax.ppermute(values, "dp", [(i, i ^ bit) for i in range(count)])


def other_row(values):
    return lax.ppermute(values, "rows", [(0, 1), (1, 0)])


def pick(values, which, axis):
    return lax.dynamic_index_in_dim(values, which, axis, keepdims=False)


def place():
    index = lax.axis_index("dp")
    return index // 4, (index // 2) % 2, index % 2


def halved_dp(slices, axis, mine, bit):
    sent = pick(slices, 1 - mine, axis).astype(jnp.bfloat16)
    return pick(slices, mine, axis) + partner(sent, bit).astype(jnp.float32)


def halved_rows(slices):
    half = slices.shape[-1] // 2
    axis = slices.ndim - 1
    mine = lax.axis_index("rows")
    sent = lax.dynamic_slice_in_dim(slices, (1 - mine) * half, half, axis=axis)
    kept = lax.dynamic_slice_in_dim(slices, mine * half, half, axis=axis)
    return kept + other_row(sent.astype(jnp.bfloat16)).astype(jnp.float32)


def in_order(mine, own, other, axis, stacked):
    first = mine == 0
    pair = [jnp.where(first, own, other), jnp.where(first, other, own)]
    return jnp.stack(pair, axis=axis) if stacked else jnp.concatenate(pair, axis=axis)


def both_rows(half):
    return in_order(lax.axis_index("rows"), half, other_row(half), half.ndim - 1, False)


def scatter_core(partial):
    line = lax.axis_size("dp") // 4
    core = place()[2]
    slices = partial.reshape(line, 2, 2, partial.shape[0] // (4 * line), partial.shape[1])
    kept = pick(slices, core, 2).astype(jnp.float32)
    return kept, partner(pick(slices, 1 - core, 2), 1).astype(jnp.float32)


def scatter_first(low, high):
    return halved_rows(low), halved_dp(high, 1, place()[1], 2)


def scatter_second(low, high):
    return jnp.concatenate([halved_dp(low, 1, place()[1], 2), halved_rows(high)], axis=0)


def scatter_line(slices):
    at = place()[0]
    total = pick(slices, at, 0)
    for step in range(1, slices.shape[0]):
        sent = pick(slices, at ^ step, 0).astype(jnp.bfloat16)
        total = total + partner(sent, 4 * step).astype(jnp.float32)
    return total


def scatter_last(half):
    return both_rows(half.astype(jnp.bfloat16)).astype(jnp.float32)


def sum_rows(slice_terms):
    sent = slice_terms.astype(jnp.bfloat16)
    return sent.astype(jnp.float32) + other_row(sent).astype(jnp.float32)


def gather_line(weight):
    line = lax.axis_size("dp") // 4
    at = place()[0]
    half = weight.shape[1] // 2
    own = lax.dynamic_slice_in_dim(weight, lax.axis_index("rows") * half, half, axis=1)
    pieces = [own] + [partner(own, 4 * step) for step in range(1, line)]
    bit = 1
    while bit < line:
        swap = (at // bit) % 2 == 1
        pieces = [jnp.where(swap, pieces[j ^ bit], pieces[j]) for j in range(line)]
        bit *= 2
    return jnp.stack(pieces[: line // 2]), jnp.stack(pieces[line // 2 :])


def gather_middle(slices):
    return in_order(place()[1], slices, partner(slices, 2), 1, True)


def gather_core(low, high):
    slices = jnp.concatenate([low, high], axis=0)
    slices = in_order(place()[2], slices, partner(slices, 1), 2, True)
    return slices.reshape(-1, slices.shape[-1])


def summed_everywhere(terms):
    flat = terms.reshape(-1, terms.shape[-1]).astype(jnp.bfloat16)
    everyone = lax.all_gather(flat, ("dp", "rows"), axis=0)
    return jnp.sum(everyone.astype(jnp.float32), axis=0).reshape(terms.shape)


def on_device(features, bucket, kernel, up_weight, down_weight, cotangent):
    images, strip_rows, canvas_cols, channels = features.shape
    rows_count = lax.axis_size("rows")
    row_index = lax.axis_index("rows")
    canvas_rows = strip_rows * rows_count
    area_cells = canvas_rows * canvas_cols // 2
    reach = kernel.shape[0] // 2
    grad_scale = 1.0 / (images * lax.axis_size("dp"))
    heights = canvas_rows // 2 + bucket
    widths = jnp.minimum(canvas_cols, area_cells // heights)
    row_ids = row_index * strip_rows + lax.iota(jnp.int32, strip_rows)
    col_ids = lax.iota(jnp.int32, canvas_cols)
    inside = (row_ids[None, :, None] < heights[:, None, None]) & (
        col_ids[None, None, :] < widths[:, None, None]
    )
    inside_cells = inside[..., None]
    masked = jnp.where(inside_cells, features, jnp.zeros((), features.dtype))
    masked_cot = jnp.where(inside_cells, cotangent, jnp.zeros((), cotangent.dtype))
    up_full = lax.all_gather(up_weight, "dp", axis=0, tiled=True)
    down_low, down_high = gather_line(down_weight)
    rimmed = padded_2(masked, (("rows", 1),), reach)
    padded = jnp.pad(rimmed, ((0, 0), (0, 0), (reach, reach), (0, 0))).astype(jnp.float32)
    padded, down_low, down_high = lax.optimization_barrier((padded, down_low, down_high))
    down_low, down_high = gather_middle(down_low), both_rows(down_high)
    convolved = depthwise(padded, kernel, strip_rows, canvas_cols, False)
    convolved, down_low, down_high = lax.optimization_barrier((convolved, down_low, down_high))
    down_low, down_high = both_rows(down_low), gather_middle(down_high)
    down_full = gather_core(down_low, down_high)
    convolved = jnp.where(inside_cells, convolved, 0.0)
    unit_norm, inv_std = layer_norm(convolved)
    normed = unit_norm.astype(jnp.bfloat16)
    tokens = normed.reshape(images * strip_rows * canvas_cols, channels)
    cot_rows = masked_cot.reshape(images * strip_rows * canvas_cols, channels)
    pre_act = jnp.dot(tokens, up_full, preferred_element_type=jnp.float32)
    hidden, derivative = gelu_parts(pre_act)
    activation = hidden.astype(jnp.bfloat16)
    down_part = (
        lax.dot_general(
            activation, cot_rows, (((0,), (0,)), ((), ())), preferred_element_type=jnp.float32
        )
        * grad_scale
    ).astype(jnp.bfloat16)
    down_kept, down_came = scatter_core(down_part)
    grad_act = lax.dot_general(
        cot_rows, down_full, (((1,), (1,)), ((), ())), preferred_element_type=jnp.float32
    )
    grad_pre = (grad_act * derivative).astype(jnp.bfloat16)
    down_part = down_kept + down_came
    grad_pre, down_part = lax.optimization_barrier((grad_pre, down_part))
    up_part = (
        lax.dot_general(
            tokens, grad_pre, (((0,), (0,)), ((), ())), preferred_element_type=jnp.float32
        )
        * grad_scale
    ).astype(jnp.bfloat16)
    up_kept, up_came = scatter_core(up_part)
    cut = up_kept.shape[0] // 2
    up_low, up_high = up_kept[:cut] + up_came[:cut], up_kept[cut:] + up_came[cut:]
    grad_rows = lax.dot_general(
        grad_pre, up_full, (((1,), (1,)), ((), ())), preferred_element_type=jnp.float32
    )
    grad_norm = grad_rows.reshape(features.shape)
    grad_conv = jnp.where(inside_cells, norm_backward(grad_norm, unit_norm, inv_std), 0.0)
    grad_conv, up_low, up_high, down_part = lax.optimization_barrier(
        (grad_conv, up_low, up_high, down_part)
    )
    grad_rimmed = padded_2(grad_conv.astype(jnp.bfloat16), (("rows", 1),), reach).astype(
        grad_conv.dtype
    )
    kernel_part = kernel_terms(grad_conv, padded, kernel.shape[0]) * grad_scale
    down_part = halved_dp(down_part, 1, place()[1], 2)
    kernel_part, grad_rimmed, up_low, up_high = lax.optimization_barrier(
        (kernel_part, grad_rimmed, up_low, up_high)
    )
    kernel_grad = summed_everywhere(kernel_part)
    up_low, up_high = scatter_first(up_low, up_high)
    grad_padded = jnp.pad(grad_rimmed, ((0, 0), (0, 0), (reach, reach), (0, 0)))
    feature_grad = jnp.where(
        inside_cells,
        masked_cot + depthwise(grad_padded, kernel, strip_rows, canvas_cols, True),
        0.0,
    ).astype(jnp.bfloat16)
    feature_grad, activation, down_part, up_low, up_high = lax.optimization_barrier(
        (feature_grad, activation, down_part, up_low, up_high)
    )
    up_part = scatter_second(up_low, up_high)
    down_part = scatter_line(down_part)
    branch = jnp.dot(activation, down_full, preferred_element_type=jnp.float32)
    block_out = (masked + branch.reshape(features.shape)).astype(jnp.bfloat16)
    block_out, up_part, down_part = lax.optimization_barrier((block_out, up_part, down_part))
    up_half = scatter_line(up_part)
    down_grad = sum_rows(down_part)
    up_grad = scatter_last(up_half)
    return (block_out, feature_grad, up_grad, down_grad, kernel_grad)


def solution(mesh):
    placed = (
        P("dp", "rows", None, None),
        P("dp"),
        P(),
        P("dp", None),
        P("dp", None),
        P("dp", "rows", None, None),
    )
    return jax.shard_map(
        on_device,
        mesh=mesh,
        in_specs=placed,
        out_specs=(
            P("dp", "rows", None, None),
            P("dp", "rows", None, None),
            P("dp", None),
            P("dp", None),
            P(),
        ),
        check_vma=False,
    )
```

```python
import functools

import jax
import jax.numpy as jnp
from jax import lax
from jax.experimental import pallas as pl
from jax.experimental.pallas import tpu as pltpu
from jax.sharding import PartitionSpec as P

INV_ROOT_TWO = 0.7071067811865476
INV_ROOT_TAU = 0.3989422804014327
EPSILON = 1e-06


def padded_2(block, sides, width):
    for axis, dim in sides:
        count = lax.axis_size(axis)
        forward = [(i, i + 1) for i in range(count - 1)]
        backward = [(target, source) for source, target in forward]
        low = lax.ppermute(
            lax.slice_in_dim(block, block.shape[dim] - width, None, axis=dim), axis, forward
        )
        high = lax.ppermute(lax.slice_in_dim(block, 0, width, axis=dim), axis, backward)
        block = jnp.concatenate([low, block, high], axis=dim)
    return block


def gelu_parts(pre_act):
    normal_cdf = 0.5 * (1.0 + lax.erf(pre_act * INV_ROOT_TWO))
    density = jnp.exp(-0.5 * pre_act * pre_act) * INV_ROOT_TAU
    return (pre_act * normal_cdf, normal_cdf + pre_act * density)


LANES = 128
SUBLANES = 8


def depthwise_kernel(flipped, padded_ref, kernel_ref, out_ref):
    span = kernel_ref.shape[0]
    rows, cols = out_ref.shape[1], out_ref.shape[2]
    for col in range(0, cols, SUBLANES):
        sums = [jnp.zeros((SUBLANES, LANES), jnp.float32)] * rows
        for start_col in range(span):
            offset_col = span - 1 - start_col if flipped else start_col
            taps = [
                jnp.broadcast_to(
                    kernel_ref[span - 1 - a if flipped else a, pl.ds(offset_col, 1), :],
                    (SUBLANES, LANES),
                )
                for a in range(span)
            ]
            for source in range(rows + span - 1):
                window = padded_ref[0, source, pl.ds(col + start_col, SUBLANES), :]
                for a in range(span):
                    if 0 <= source - a < rows:
                        sums[source - a] = sums[source - a] + taps[a] * window
        for row in range(rows):
            out_ref[0, row, pl.ds(col, SUBLANES), :] = sums[row]


def depthwise(padded, kernel, out_rows, out_cols, flipped):
    images, channels = padded.shape[0], padded.shape[-1]
    span = kernel.shape[0]
    taps = span * span * out_rows * out_cols * channels * images
    return pl.pallas_call(
        functools.partial(depthwise_kernel, flipped),
        grid=(images, channels // LANES),
        in_specs=[
            pl.BlockSpec((1,) + padded.shape[1:3] + (LANES,), lambda i, c: (i, 0, 0, c)),
            pl.BlockSpec((span, span, LANES), lambda i, c: (0, 0, c)),
        ],
        out_specs=pl.BlockSpec((1, out_rows, out_cols, LANES), lambda i, c: (i, 0, 0, c)),
        out_shape=jax.ShapeDtypeStruct((images, out_rows, out_cols, channels), jnp.float32),
        cost_estimate=pl.CostEstimate(
            flops=2 * taps, bytes_accessed=4 * padded.size, transcendentals=0
        ),
        compiler_params=pltpu.CompilerParams(vmem_limit_bytes=16 * 1024 * 1024),
    )(padded.astype(jnp.float32), kernel)


def kernel_terms_kernel(span, grad_ref, padded_ref, out_ref):
    rows, cols = grad_ref.shape[1], grad_ref.shape[2]
    for col in range(0, cols, SUBLANES):
        grads = [grad_ref[0, row, pl.ds(col, SUBLANES), :] for row in range(rows)]
        for offset_col in range(span):
            sums = [jnp.zeros((SUBLANES, LANES), jnp.float32)] * span
            for source in range(rows + span - 1):
                window = padded_ref[0, source, pl.ds(col + offset_col, SUBLANES), :]
                for a in range(span):
                    if 0 <= source - a < rows:
                        sums[a] = sums[a] + grads[source - a] * window
            for a in range(span):
                if col == 0:
                    out_ref[0, a * span + offset_col] = sums[a]
                else:
                    out_ref[0, a * span + offset_col] += sums[a]


def kernel_terms(grad_conv, padded, span):
    images, rows, cols, channels = grad_conv.shape
    taps = span * span * grad_conv.size
    terms = pl.pallas_call(
        functools.partial(kernel_terms_kernel, span),
        grid=(images, channels // LANES),
        in_specs=[
            pl.BlockSpec((1, rows, cols, LANES), lambda i, c: (i, 0, 0, c)),
            pl.BlockSpec((1,) + padded.shape[1:3] + (LANES,), lambda i, c: (i, 0, 0, c)),
        ],
        out_specs=pl.BlockSpec((1, span * span, SUBLANES, LANES), lambda i, c: (i, 0, 0, c)),
        out_shape=jax.ShapeDtypeStruct((images, span * span, SUBLANES, channels), jnp.float32),
        cost_estimate=pl.CostEstimate(
            flops=2 * taps, bytes_accessed=4 * padded.size, transcendentals=0
        ),
        compiler_params=pltpu.CompilerParams(vmem_limit_bytes=16 * 1024 * 1024),
    )(grad_conv, padded.astype(jnp.float32))
    return jnp.sum(terms, axis=(0, 2)).reshape(span, span, channels)


def layer_norm(convolved):
    centered = convolved - jnp.mean(convolved, axis=-1, keepdims=True)
    inv_std = lax.rsqrt(jnp.mean(centered * centered, axis=-1, keepdims=True) + EPSILON)
    return (centered * inv_std, inv_std)


def norm_backward(grad_norm, unit_norm, inv_std):
    first_mean = jnp.mean(grad_norm, axis=-1, keepdims=True)
    second_mean = jnp.mean(grad_norm * unit_norm, axis=-1, keepdims=True)
    return inv_std * (grad_norm - first_mean - unit_norm * second_mean)


def partner(values, bit):
    count = lax.axis_size("dp")
    return lax.ppermute(values, "dp", [(i, i ^ bit) for i in range(count)])


def other_row(values):
    return lax.ppermute(values, "rows", [(0, 1), (1, 0)])


def pick(values, which, axis):
    return lax.dynamic_index_in_dim(values, which, axis, keepdims=False)


def place():
    index = lax.axis_index("dp")
    return index // 4, (index // 2) % 2, index % 2


def halved_dp(slices, axis, mine, bit):
    sent = pick(slices, 1 - mine, axis).astype(jnp.bfloat16)
    return pick(slices, mine, axis) + partner(sent, bit).astype(jnp.float32)


def halved_rows(slices):
    half = slices.shape[-1] // 2
    axis = slices.ndim - 1
    mine = lax.axis_index("rows")
    sent = lax.dynamic_slice_in_dim(slices, (1 - mine) * half, half, axis=axis)
    kept = lax.dynamic_slice_in_dim(slices, mine * half, half, axis=axis)
    return kept + other_row(sent.astype(jnp.bfloat16)).astype(jnp.float32)


def in_order(mine, own, other, axis, stacked):
    first = mine == 0
    pair = [jnp.where(first, own, other), jnp.where(first, other, own)]
    return jnp.stack(pair, axis=axis) if stacked else jnp.concatenate(pair, axis=axis)


def both_rows(half):
    return in_order(lax.axis_index("rows"), half, other_row(half), half.ndim - 1, False)


def scatter_core(partial):
    line = lax.axis_size("dp") // 4
    core = place()[2]
    slices = partial.reshape(line, 2, 2, partial.shape[0] // (4 * line), partial.shape[1])
    kept = pick(slices, core, 2).astype(jnp.float32)
    return kept, partner(pick(slices, 1 - core, 2), 1).astype(jnp.float32)


def scatter_first(low, high):
    return halved_rows(low), halved_dp(high, 1, place()[1], 2)


def scatter_second(low, high):
    return jnp.concatenate([halved_dp(low, 1, place()[1], 2), halved_rows(high)], axis=0)


def scatter_line(slices):
    at = place()[0]
    total = pick(slices, at, 0)
    for step in range(1, slices.shape[0]):
        sent = pick(slices, at ^ step, 0).astype(jnp.bfloat16)
        total = total + partner(sent, 4 * step).astype(jnp.float32)
    return total


def scatter_last(half):
    return both_rows(half.astype(jnp.bfloat16)).astype(jnp.float32)


def sum_rows(slice_terms):
    sent = slice_terms.astype(jnp.bfloat16)
    return sent.astype(jnp.float32) + other_row(sent).astype(jnp.float32)


def gather_line(weight):
    line = lax.axis_size("dp") // 4
    at = place()[0]
    half = weight.shape[1] // 2
    own = lax.dynamic_slice_in_dim(weight, lax.axis_index("rows") * half, half, axis=1)
    pieces = [own] + [partner(own, 4 * step) for step in range(1, line)]
    bit = 1
    while bit < line:
        swap = (at // bit) % 2 == 1
        pieces = [jnp.where(swap, pieces[j ^ bit], pieces[j]) for j in range(line)]
        bit *= 2
    return jnp.stack(pieces[: line // 2]), jnp.stack(pieces[line // 2 :])


def gather_middle(slices):
    return in_order(place()[1], slices, partner(slices, 2), 1, True)


def gather_core(low, high):
    slices = jnp.concatenate([low, high], axis=0)
    slices = in_order(place()[2], slices, partner(slices, 1), 2, True)
    return slices.reshape(-1, slices.shape[-1])


def summed_line(values):
    line = lax.axis_size("dp") // 4
    at = place()[0]
    pieces = [values] + [partner(values, 4 * step) for step in range(1, line)]
    bit = 1
    while bit < line:
        swap = (at // bit) % 2 == 1
        pieces = [jnp.where(swap, pieces[j ^ bit], pieces[j]) for j in range(line)]
        bit *= 2
    return functools.reduce(jnp.add, pieces)


def on_device(features, bucket, kernel, up_weight, down_weight, cotangent):
    images, strip_rows, canvas_cols, channels = features.shape
    rows_count = lax.axis_size("rows")
    row_index = lax.axis_index("rows")
    canvas_rows = strip_rows * rows_count
    area_cells = canvas_rows * canvas_cols // 2
    reach = kernel.shape[0] // 2
    grad_scale = 1.0 / (images * lax.axis_size("dp"))
    heights = canvas_rows // 2 + bucket
    widths = jnp.minimum(canvas_cols, area_cells // heights)
    row_ids = row_index * strip_rows + lax.iota(jnp.int32, strip_rows)
    col_ids = lax.iota(jnp.int32, canvas_cols)
    inside = (row_ids[None, :, None] < heights[:, None, None]) & (
        col_ids[None, None, :] < widths[:, None, None]
    )
    inside_cells = inside[..., None]
    masked = jnp.where(inside_cells, features, jnp.zeros((), features.dtype))
    masked_cot = jnp.where(inside_cells, cotangent, jnp.zeros((), cotangent.dtype))
    up_full = lax.all_gather(up_weight, "dp", axis=0, tiled=True)
    down_low, down_high = gather_line(down_weight)
    rimmed = padded_2(masked, (("rows", 1),), reach)
    padded = jnp.pad(rimmed, ((0, 0), (0, 0), (reach, reach), (0, 0))).astype(jnp.float32)
    padded, down_low, down_high = lax.optimization_barrier((padded, down_low, down_high))
    down_low, down_high = gather_middle(down_low), both_rows(down_high)
    convolved = depthwise(padded, kernel, strip_rows, canvas_cols, False)
    convolved, down_low, down_high = lax.optimization_barrier((convolved, down_low, down_high))
    down_low, down_high = both_rows(down_low), gather_middle(down_high)
    down_full = gather_core(down_low, down_high)
    convolved = jnp.where(inside_cells, convolved, 0.0)
    unit_norm, inv_std = layer_norm(convolved)
    normed = unit_norm.astype(jnp.bfloat16)
    tokens = normed.reshape(images * strip_rows * canvas_cols, channels)
    cot_rows = masked_cot.reshape(images * strip_rows * canvas_cols, channels)
    pre_act = jnp.dot(tokens, up_full, preferred_element_type=jnp.float32)
    hidden, derivative = gelu_parts(pre_act)
    activation = hidden.astype(jnp.bfloat16)
    down_part = (
        lax.dot_general(
            activation, cot_rows, (((0,), (0,)), ((), ())), preferred_element_type=jnp.float32
        )
        * grad_scale
    ).astype(jnp.bfloat16)
    down_kept, down_came = scatter_core(down_part)
    grad_act = lax.dot_general(
        cot_rows, down_full, (((1,), (1,)), ((), ())), preferred_element_type=jnp.float32
    )
    grad_pre = (grad_act * derivative).astype(jnp.bfloat16)
    down_part = down_kept + down_came
    grad_pre, down_part = lax.optimization_barrier((grad_pre, down_part))
    up_part = (
        lax.dot_general(
            tokens, grad_pre, (((0,), (0,)), ((), ())), preferred_element_type=jnp.float32
        )
        * grad_scale
    ).astype(jnp.bfloat16)
    up_kept, up_came = scatter_core(up_part)
    cut = up_kept.shape[0] // 2
    up_low, up_high = up_kept[:cut] + up_came[:cut], up_kept[cut:] + up_came[cut:]
    grad_rows = lax.dot_general(
        grad_pre, up_full, (((1,), (1,)), ((), ())), preferred_element_type=jnp.float32
    )
    grad_norm = grad_rows.reshape(features.shape)
    grad_conv = jnp.where(inside_cells, norm_backward(grad_norm, unit_norm, inv_std), 0.0)
    grad_conv, up_low, up_high = lax.optimization_barrier((grad_conv, up_low, up_high))
    grad_rimmed = padded_2(grad_conv.astype(jnp.bfloat16), (("rows", 1),), reach).astype(
        grad_conv.dtype
    )
    kernel_part = kernel_terms(grad_conv, padded, kernel.shape[0]) * grad_scale
    down_part = halved_dp(down_part, 1, place()[1], 2)
    kernel_part, grad_rimmed, up_low, up_high, down_part = lax.optimization_barrier(
        (kernel_part, grad_rimmed, up_low, up_high, down_part)
    )
    kernel_part = kernel_part + partner(kernel_part, 1)
    down_part = scatter_line(down_part)
    up_low, up_high = scatter_first(up_low, up_high)
    grad_padded = jnp.pad(grad_rimmed, ((0, 0), (0, 0), (reach, reach), (0, 0)))
    feature_grad = jnp.where(
        inside_cells,
        masked_cot + depthwise(grad_padded, kernel, strip_rows, canvas_cols, True),
        0.0,
    ).astype(jnp.bfloat16)
    feature_grad, activation, down_part, up_low, up_high, kernel_part = lax.optimization_barrier(
        (feature_grad, activation, down_part, up_low, up_high, kernel_part)
    )
    up_part = scatter_second(up_low, up_high)
    kernel_part = kernel_part + partner(kernel_part, 2)
    branch = jnp.dot(activation, down_full, preferred_element_type=jnp.float32)
    block_out = (masked + branch.reshape(features.shape)).astype(jnp.bfloat16)
    block_out, up_part, kernel_part = lax.optimization_barrier((block_out, up_part, kernel_part))
    kernel_grad = summed_line(kernel_part + other_row(kernel_part))
    up_half = scatter_line(up_part)
    down_grad = sum_rows(down_part)
    up_grad = scatter_last(up_half)
    return (block_out, feature_grad, up_grad, down_grad, kernel_grad)


def solution(mesh):
    placed = (
        P("dp", "rows", None, None),
        P("dp"),
        P(),
        P("dp", None),
        P("dp", None),
        P("dp", "rows", None, None),
    )
    return jax.shard_map(
        on_device,
        mesh=mesh,
        in_specs=placed,
        out_specs=(
            P("dp", "rows", None, None),
            P("dp", "rows", None, None),
            P("dp", None),
            P("dp", None),
            P(),
        ),
        check_vma=False,
    )
```
